32 devices in a mesh: kpool: 2 (over x), fft: 16 (over z, y, core).
Axes of the slice: x: 2, y: 2, z: 4, core: 2. Of those that a mesh axis runs over, the one named last changes fastest.
Arguments:
- orbitals: float32 [2, 8, 4, 4096], P('kpool', None, None, 'fft'), may hold values from -6 to 6
- response: float32 [2, 8, 4, 4096], P('kpool', None, None, 'fft'), may hold values from -6 to 6
- residual: float32 [2, 8, 4, 4096], P('kpool', None, None, 'fft'), may hold values from -9 to 9
- old_direction: float32 [2, 8, 4, 4096], P('kpool', None, None, 'fft'), may hold values from -6 to 6
- old_norm: float32 [2, 8], P('kpool'), may hold values from 2457.6 to 1802240
- band_energy: float32 [2, 8], P('kpool'), may hold values from -1 to 0.4
- kinetic: float32 [2, 4096], P('kpool', 'fft'), may hold values from 0.5 to 20
- form_factor: float32 [2, 2, 16, 4096], P('kpool', None, None, 'fft'), may hold values from -0.09375 to 0.09375
- sphere_index: int32 [2, 4096], P('kpool', 'fft'), may hold values from 0 to 262143, as said below
- atom_positions: float32 [3, 64], replicated, may hold values from 0 to 1
- proj_atom: int32 [1024], replicated, may hold values from 0 to 63
- coupling: float32 [2, 32, 32], replicated, may hold values from -0.03 to 3
- potential: float32 [4, 64, 4096], P(None, 'fft'), may hold values from -0.3 to 2
Outputs:
- response_next: float32 [2, 8, 4, 4096], P('kpool', None, None, 'fft')
- residual_next: float32 [2, 8, 4, 4096], P('kpool', None, None, 'fft')
- direction: float32 [2, 8, 4, 4096], P('kpool', None, None, 'fft')
- induced_density: float32 [4, 64, 4096], P(None, 'fft')
The draws below stay inside these ranges and needn't reach their ends.
Inputs may be any that keep to these rules, and one draw needn't show every extreme that they name: `sphere_index`: within one point the entries are distinct. Entry j = b * 32 + t (t < 32) has gz = (t - 16) mod 64, and the 32 entries of one b share one column (gx, gy), so the plane waves of every device are whole columns. The columns of one point are the 128 columns nearest the anchor in signed frequencies f(gx)^2 + f(gy)^2, ties broken at random, in a random order.
All inputs are finite; a program needn't handle non-finite values.
Results may differ from the reference program's by a relative error of at most 0.0003.
Values sent between devices are 32-bit elements; how exact they have to be, the bound alone decides.
A program may use at most 128 MiB of HBM per device.

```python
import math
import jax
import jax.numpy as jnp
from jax import lax

NG = 64
NB = 8
NK = 2
STICK_LEN = 32
NPW = 4096
NATOM = 64
PA = 16
NPROJ = 1024


def band_scales(key):
    return jnp.exp(jax.random.uniform(jax.random.fold_in(key, 5), (NK, NB), jnp.float32, math.log(0.3), math.log(3.0)))


def draw_residual(key, part):
    scales = band_scales(key)
    key = jax.random.fold_in(key, 15)
    first = jax.random.fold_in(key, 0)
    ramp = jnp.exp(math.log(3.0) * jnp.arange(NPW, dtype=jnp.float32) / max(NPW - 1, 1))
    noise = jax.random.uniform(first, (NK, NB, 4, NPW), jnp.float32, -1.0, 1.0)
    return noise * ramp[None, None, None, :] * scales[:, :, None, None]


def draw_old_norm(key, part):
    scales = band_scales(key)
    key = jax.random.fold_in(key, 16)
    factor = jnp.exp(jax.random.uniform(key, (NK, NB), jnp.float32, math.log(1.5), math.log(10.0)))
    return scales * scales * (4.85 * NPW) * factor


def draw_sphere_index(key, part):
    key = jax.random.fold_in(key, 11)
    columns = NPW // STICK_LEN
    cells = jnp.arange(NG * NG, dtype=jnp.int32)
    half = NG // 2
    col_x = cells // NG
    col_y = cells % NG
    signed_x = jnp.where(col_x < half, col_x, col_x - NG)
    signed_y = jnp.where(col_y < half, col_y, col_y - NG)
    radius = signed_x * signed_x + signed_y * signed_y
    depth = (jnp.arange(STICK_LEN, dtype=jnp.int32) - STICK_LEN // 2) % NG
    keys = jax.random.split(key, NK)

    def one_point(point_key):
        first, second = jax.random.split(point_key)
        tiebreak = jax.random.permutation(first, NG * NG).astype(jnp.int32)
        score = radius * (NG * NG) + tiebreak
        chosen = jnp.argsort(score, stable=True)[:columns].astype(jnp.int32)
        shuffled = jnp.take(chosen, jax.random.permutation(second, columns).astype(jnp.int32))
        return (shuffled[:, None] * NG + depth[None, :]).reshape(NPW).astype(jnp.int32)
    return jax.vmap(one_point)(keys)


def draw_coupling(key, part):
    key = jax.random.fold_in(key, 13)
    first, second = jax.random.split(key)
    width = 2 * PA
    offdiag = jax.random.uniform(first, (2, width, width), jnp.float32, -0.03, 0.03)
    diagonal = jax.random.uniform(second, (width,), jnp.float32, 1.5, 3.0)
    steps = jnp.arange(width, dtype=jnp.int32)
    unit = (steps[:, None] == steps[None, :]).astype(jnp.float32)
    real_part = offdiag[0] * (1.0 - unit) + unit * diagonal[None, :]
    imag_part = offdiag[1] * (1.0 - unit)
    return jnp.stack([real_part, imag_part])


def draw_potential(key, part):
    key = jax.random.fold_in(key, 14)
    first, second = jax.random.split(key)
    shape = (NG, NG * NG)
    base = jax.random.uniform(first, shape, jnp.float32, 1.0, 2.0)
    field = jax.random.uniform(second, (3,) + shape, jnp.float32, -0.3, 0.3)
    return jnp.concatenate([base[None], field], axis=0)


def place_ends(entries, key, least, high):
    longest = entries.shape.index(max(entries.shape))
    spots = []
    for shift in (0, 1):
        where = [jax.random.randint(jax.random.fold_in(key, axis), (), 0, length) for axis, length in enumerate(entries.shape)]
        where[longest] = (where[longest] + shift) % entries.shape[longest]
        spots.append(tuple(where))
    return entries.at[spots[0]].set(least).at[spots[1]].set(high)


def shard_levels(key, dims, cuts, least, largest):
    loudness, own = 1.0, jax.random.fold_in(key, 6)
    for dim, parts in cuts:
        draws = jnp.exp(jax.random.uniform(jax.random.fold_in(own, dim), (parts,), jnp.float32, least / len(cuts), largest / len(cuts)))
        loudness = loudness * jnp.repeat(draws, dims[dim] // parts).reshape([-1 if axis == dim else 1 for axis in range(len(dims))])
    return loudness


def scatter_about(stream_key, shape, scale, limit, cuts=(), held_as=jnp.bfloat16):
    array = scale * jax.random.normal(stream_key, shape, jnp.float32)
    if cuts:
        array = array * shard_levels(stream_key, shape, cuts, -0.22, 0.18)
    return jnp.clip(array, -limit, limit).astype(held_as)


def setup_inputs(seed: int = 0) -> dict:
    splits = jax.random.split(jax.random.key(seed), 14)
    return {
        "orbitals": scatter_about(splits[0], (NK, NB, 4, NPW), 1.0, 6.0, ((0, 2), (3, 16)), jnp.float32),
        "response": scatter_about(splits[1], (NK, NB, 4, NPW), 1.0, 6.0, ((0, 2), (3, 16)), jnp.float32),
        "residual": draw_residual(jax.random.fold_in(splits[13], 71), 0),
        "old_direction": scatter_about(splits[3], (NK, NB, 4, NPW), 1.0, 6.0, ((0, 2), (3, 16)), jnp.float32),
        "old_norm": draw_old_norm(jax.random.fold_in(splits[13], 71), 0),
        "band_energy": jnp.clip(-1.0 + 1.4 * jax.random.uniform(splits[5], (NK, NB), jnp.float32) ** shard_levels(splits[5], (NK, NB), ((0, 2),), -0.2, 0.2), -1.0, 0.4),
        "kinetic": jnp.clip(jnp.exp(math.log(20.0) - 3.6888795 * jax.random.uniform(splits[6], (NK, NPW), jnp.float32) ** shard_levels(splits[6], (NK, NPW), ((0, 2), (1, 16)), -0.2, 0.2)), 0.5, 20.0),
        "form_factor": scatter_about(splits[7], (NK, 2, PA, NPW), NPW ** -0.5, 0.09375, ((0, 2), (3, 16)), jnp.float32),
        "sphere_index": draw_sphere_index(jax.random.fold_in(splits[13], 71), 0),
        "atom_positions": jnp.clip(jax.random.uniform(splits[9], (3, NATOM), jnp.float32, 0.0, 1.0), 0.0, 1.0),
        "proj_atom": place_ends(jax.random.randint(splits[10], (NPROJ,), 0, NATOM), jax.random.fold_in(splits[10], 1), 0, NATOM - 1).astype(jnp.int32),
        "coupling": draw_coupling(jax.random.fold_in(splits[13], 71), 0),
        "potential": draw_potential(jax.random.fold_in(splits[13], 71), 0),
    }


TWO_PI = 2.0 * math.pi
SMALL_TERM = 1e-6
HIGHEST = lax.Precision.HIGHEST


def contract(form_text, *operands):
    return jnp.einsum(form_text, *operands, precision=HIGHEST)


def frequencies(index, length):
    def signed(values):
        return jnp.where(values < length // 2, values, values - length).astype(jnp.float32)
    return signed(index // (length * length)), signed((index // length) % length), signed(index % length)


def projector_tables(form_factor, sphere_index, atom_positions, proj_atom, length):
    freq_x, freq_y, freq_z = frequencies(sphere_index, length)
    theta = TWO_PI * (atom_positions[0][:, None] * freq_x[None, :] + atom_positions[1][:, None] * freq_y[None, :] + atom_positions[2][:, None] * freq_z[None, :])
    cosine = jnp.cos(theta)
    sine = jnp.sin(theta)
    channels = form_factor.shape[1]
    slots = proj_atom.reshape(channels, -1)
    cos_rows = jnp.take(cosine, slots, axis=0)
    sin_rows = jnp.take(sine, slots, axis=0)
    real_part = form_factor[0][:, None, :]
    imag_part = form_factor[1][:, None, :]
    return real_part * cos_rows + imag_part * sin_rows, imag_part * cos_rows - real_part * sin_rows


def project(values, tab_real, tab_imag):
    val_real = values[:, 0::2]
    val_imag = values[:, 1::2]
    amp_real = contract('ckg,nsg->sckn', tab_real, val_real) + contract('ckg,nsg->sckn', tab_imag, val_imag)
    amp_imag = contract('ckg,nsg->sckn', tab_real, val_imag) - contract('ckg,nsg->sckn', tab_imag, val_real)
    return amp_real, amp_imag


def combine(amp_real, amp_imag, proj_atom, coupling):
    channels = amp_real.shape[1]
    atoms = amp_real.shape[2]
    slots = proj_atom.reshape(channels, atoms)
    onehot = (slots[:, None, :] == jnp.arange(atoms, dtype=jnp.int32)[None, :, None]).astype(amp_real.dtype)
    by_real = contract('cak,sckn->scan', onehot, amp_real)
    by_imag = contract('cak,sckn->scan', onehot, amp_imag)
    herm_real = (0.5 * (coupling[0] + coupling[0].T)).reshape(2, channels, 2, channels)
    herm_imag = (0.5 * (coupling[1] - coupling[1].T)).reshape(2, channels, 2, channels)
    out_real = contract('scte,tean->scan', herm_real, by_real) - contract('scte,tean->scan', herm_imag, by_imag)
    out_imag = contract('scte,tean->scan', herm_real, by_imag) + contract('scte,tean->scan', herm_imag, by_real)
    return contract('cak,scan->sckn', onehot, out_real), contract('cak,scan->sckn', onehot, out_imag)


def expand(q_real, q_imag, tab_real, tab_imag):
    new_real = contract('ckg,sckn->nsg', tab_real, q_real) - contract('ckg,sckn->nsg', tab_imag, q_imag)
    new_imag = contract('ckg,sckn->nsg', tab_real, q_imag) + contract('ckg,sckn->nsg', tab_imag, q_real)
    bands, points = new_real.shape[0], new_real.shape[2]
    return jnp.stack([new_real, new_imag], axis=2).reshape(bands, 4, points)


def apply_potential(values, potential):
    up_re, up_im, down_re, down_im = values[:, 0], values[:, 1], values[:, 2], values[:, 3]
    scalar, field_x, field_y, field_z = potential[0], potential[1], potential[2], potential[3]
    upper = scalar + field_z
    lower = scalar - field_z
    new_up_re = upper * up_re + field_x * down_re + field_y * down_im
    new_up_im = upper * up_im + field_x * down_im - field_y * down_re
    new_down_re = field_x * up_re - field_y * up_im + lower * down_re
    new_down_im = field_x * up_im + field_y * up_re + lower * down_im
    return jnp.stack([new_up_re, new_up_im, new_down_re, new_down_im], axis=1)


def density_terms(orbital, changed):
    up_re, up_im, down_re, down_im = orbital[:, 0], orbital[:, 1], orbital[:, 2], orbital[:, 3]
    ch_up_re, ch_up_im, ch_down_re, ch_down_im = changed[:, 0], changed[:, 1], changed[:, 2], changed[:, 3]
    same_up = up_re * ch_up_re + up_im * ch_up_im
    same_down = down_re * ch_down_re + down_im * ch_down_im
    charge = 2.0 * (same_up + same_down)
    spin_x = 2.0 * (up_re * ch_down_re + up_im * ch_down_im + down_re * ch_up_re + down_im * ch_up_im)
    spin_y = 2.0 * ((up_re * ch_down_im - up_im * ch_down_re) - (down_re * ch_up_im - down_im * ch_up_re))
    spin_z = 2.0 * (same_up - same_down)
    return jnp.stack([jnp.sum(charge, axis=0), jnp.sum(spin_x, axis=0), jnp.sum(spin_y, axis=0), jnp.sum(spin_z, axis=0)])


def to_real(coefficients, sphere_index):
    complex_values = lax.complex(coefficients[0::2], coefficients[1::2])
    box = jnp.zeros((2, NG * NG * NG), complex_values.dtype).at[:, sphere_index].set(complex_values)
    grid_values = jnp.fft.ifftn(box.reshape(2, NG, NG, NG), axes=(1, 2, 3)) * (NG * NG * NG)
    grid_values = jnp.transpose(grid_values, (0, 3, 1, 2)).reshape(2, NG, NG * NG)
    return jnp.stack([grid_values.real, grid_values.imag], axis=1).reshape(4, NG, NG * NG)


def to_recip(values, sphere_index):
    complex_values = lax.complex(values[0::2], values[1::2]).reshape(2, NG, NG, NG)
    complex_values = jnp.transpose(complex_values, (0, 2, 3, 1))
    spectrum = jnp.fft.fftn(complex_values, axes=(1, 2, 3)).reshape(2, NG * NG * NG) / (NG * NG * NG)
    picked = jnp.take(spectrum, sphere_index, axis=1)
    return jnp.stack([picked.real, picked.imag], axis=1).reshape(4, -1)


def one_point(orbitals, response, residual, old_direction, old_norm, band_energy, kinetic, form_factor, sphere_index, atom_positions, proj_atom, coupling, potential):
    norm_now = jnp.sum(residual * residual, axis=(1, 2))
    ratio = norm_now / old_norm
    direction = residual + ratio[:, None, None] * old_direction
    tab_real, tab_imag = projector_tables(form_factor, sphere_index, atom_positions, proj_atom, NG)
    amp_real, amp_imag = project(direction, tab_real, tab_imag)
    q_real, q_imag = combine(amp_real, amp_imag, proj_atom, coupling)
    nonlocal_term = expand(q_real, q_imag, tab_real, tab_imag)

    def potential_band(coefficients):
        grid_values = to_real(coefficients, sphere_index)
        return to_recip(apply_potential(grid_values[None], potential)[0], sphere_index)

    potential_term = lax.map(potential_band, direction)
    image = kinetic[None, None, :] * direction + potential_term + nonlocal_term - band_energy[:, None, None] * direction
    curvature = jnp.sum(direction * image, axis=(1, 2))
    step = norm_now / (curvature + SMALL_TERM)

    def density_band(total, items):
        coef_orbital, coef_response, coef_direction, band_step = items
        changed = to_real(coef_response, sphere_index) + band_step * to_real(coef_direction, sphere_index)
        return total + density_terms(to_real(coef_orbital, sphere_index)[None], changed[None]), None

    density, _ = lax.scan(density_band, jnp.zeros((4, NG, NG * NG), jnp.float32), (orbitals, response, direction, step))
    return response + step[:, None, None] * direction, residual - step[:, None, None] * image, direction, density


def reference(orbitals, response, residual, old_direction, old_norm, band_energy, kinetic, form_factor, sphere_index, atom_positions, proj_atom, coupling, potential):
    next_response, next_residual, directions = [], [], []
    density = jnp.zeros((4, NG, NG * NG), jnp.float32)
    for point in range(NK):
        result = one_point(orbitals[point], response[point], residual[point], old_direction[point], old_norm[point], band_energy[point], kinetic[point], form_factor[point], sphere_index[point], atom_positions, proj_atom, coupling, potential)
        next_response.append(result[0])
        next_residual.append(result[1])
        directions.append(result[2])
        density = density + result[3]
    density = density / (NK * NPW)
    return jnp.stack(next_response), jnp.stack(next_residual), jnp.stack(directions), density
```

```python
import functools
import math

import jax
import jax.numpy as jnp
import numpy as np
from jax import lax
from jax.experimental import pallas as pl
from jax.experimental.pallas import tpu as pltpu
from jax.sharding import PartitionSpec as P

NG = 64
STICK_LEN = 32

TWO_PI = 2.0 * math.pi
SMALL_TERM = 1e-06
HIGH = lax.Precision.HIGH


def contract(form_text, *operands):
    return jnp.einsum(form_text, *operands, precision=HIGH)


def line_matrix(columns):
    depth = (np.arange(STICK_LEN) - STICK_LEN // 2) % NG
    angle = 2.0 * np.pi / NG * (np.outer(np.arange(NG), depth) % NG)
    cosine, sine = np.cos(angle), np.sin(angle)
    parts = np.stack([np.stack([cosine, -sine], 1), np.stack([sine, cosine], 1)], 1)
    full = np.einsum("zdct,SR->zdScRt", parts, np.eye(columns))
    return full.reshape(NG * 2 * columns, 2 * columns * STICK_LEN).astype(np.float32)


def signed(values):
    return jnp.where(values < NG // 2, values, values - NG).astype(jnp.float32)


def column_phases(col_x, col_y):
    steps = jnp.arange(2 * NG, dtype=jnp.int32)
    wound = (col_x[:, None] * (steps // NG)[None, :] + col_y[:, None] * (steps % NG)[None, :]) % NG
    turn = jnp.broadcast_to(2 * col_x[:, None] % NG, wound.shape)
    angle = TWO_PI / NG * jnp.stack([wound, turn]).astype(jnp.float32)
    return jnp.stack([jnp.cos(angle), jnp.sin(angle)], 1)


def split(values):
    high = values.astype(jnp.bfloat16)
    return high, (values - high.astype(jnp.float32)).astype(jnp.bfloat16)


def product(left, right, dims):
    def one(a, b):
        return lax.dot_general(a, b, (dims, ((), ())), preferred_element_type=jnp.float32)

    return one(left[0], right[0]) + (one(left[0], right[1]) + one(left[1], right[0]))


def planes_kernel(
    slab, bands, values_ref, phase_ref, potential_ref,
    sticks_ref, curve_ref, base_ref, slope_ref,
    carry, high, low,
):
    count = phase_ref.shape[2]
    tile = potential_ref.shape[2]

    @pl.when(pl.program_id(0) == 0)
    def _():
        carry[...] = phase_ref[0]
        sticks_ref[...] = jnp.zeros_like(sticks_ref)
        curve_ref[...] = jnp.zeros_like(curve_ref)

    for pair in range(tile // (2 * NG)):
        cosine, sine = carry[0], carry[1]
        first, second = pair * 2 * NG, tile + pair * 2 * NG
        cos_parts, sin_parts = split(cosine), split(sine)
        for out, c, s in zip((high, low), cos_parts, sin_parts):
            out[0:count, first : first + 2 * NG] = c
            out[0:count, second : second + 2 * NG] = s
            out[count:, first : first + 2 * NG] = -s
            out[count:, second : second + 2 * NG] = c
        turn_c, turn_s = phase_ref[1, 0], phase_ref[1, 1]
        carry[0] = cosine * turn_c - sine * turn_s
        carry[1] = sine * turn_c + cosine * turn_s

    table = (high[...], low[...])
    grid = product(split(values_ref[...]), table, ((1,), (0,)))
    total = jnp.zeros((bands, tile), jnp.float32)
    fields = []
    for z in range(slab):

        def part(field, spin):
            row = ((z * 3 + field) * 2 + spin) * bands
            block = grid[row : row + bands]
            return block[:, :tile], block[:, tile:]

        (ur, ui), (dr, di) = part(0, 0), part(0, 1)

        def terms(up, down):
            (pr, pi), (qr, qi) = up, down
            same_up = ur * pr + ui * pi
            same_down = dr * qr + di * qi
            return (
                same_up + same_down,
                ur * qr + ui * qi + dr * pr + di * pi,
                ur * qi - ui * qr - (dr * pi - di * pr),
                same_up - same_down,
            )

        (pr, pi), (qr, qi) = part(2, 0), part(2, 1)
        for mu, value in enumerate(terms(part(1, 0), part(1, 1))):
            base_ref[mu, z : z + 1, :] = jnp.sum(value, axis=0, keepdims=True)
        for mu, value in enumerate(terms((pr, pi), (qr, qi))):
            slope_ref[mu, z] = value
        scalar, bx, by, bz = (potential_ref[k, z : z + 1, :] for k in range(4))
        upper, lower = scalar + bz, scalar - bz
        new_pr = upper * pr + bx * qr + by * qi
        new_pi = upper * pi + bx * qi - by * qr
        new_qr = bx * pr - by * pi + lower * qr
        new_qi = bx * pi + by * pr + lower * qi
        total = total + (pr * new_pr + pi * new_pi + qr * new_qr + qi * new_qi)
        fields.append(jnp.concatenate([new_pr, new_pi], axis=1))
        fields.append(jnp.concatenate([new_qr, new_qi], axis=1))
    sticks_ref[...] += product(split(jnp.concatenate(fields, axis=0)), table, ((1,), (1,)))
    curve_ref[...] += total


def planes(values, phases, potential, bands):
    slab, cells = potential.shape[1], potential.shape[2]
    count = phases.shape[2]
    tile = 8 * NG
    return pl.pallas_call(
        functools.partial(planes_kernel, slab, bands),
        grid=(cells // tile,),
        in_specs=[
            pl.BlockSpec(values.shape, lambda i: (0, 0)),
            pl.BlockSpec(phases.shape, lambda i: (0, 0, 0, 0)),
            pl.BlockSpec((4, slab, tile), lambda i: (0, 0, i)),
        ],
        out_specs=[
            pl.BlockSpec((slab * 2 * bands, 2 * count), lambda i: (0, 0)),
            pl.BlockSpec((bands, tile), lambda i: (0, 0)),
            pl.BlockSpec((4, slab, tile), lambda i: (0, 0, i)),
            pl.BlockSpec((4, slab, bands, tile), lambda i: (0, 0, 0, i)),
        ],
        out_shape=[
            jax.ShapeDtypeStruct((slab * 2 * bands, 2 * count), jnp.float32),
            jax.ShapeDtypeStruct((bands, tile), jnp.float32),
            jax.ShapeDtypeStruct((4, slab, cells), jnp.float32),
            jax.ShapeDtypeStruct((4, slab, bands, cells), jnp.float32),
        ],
        scratch_shapes=[
            pltpu.VMEM((2, count, 2 * NG), jnp.float32),
            pltpu.VMEM((2 * count, 2 * tile), jnp.bfloat16),
            pltpu.VMEM((2 * count, 2 * tile), jnp.bfloat16),
        ],
        compiler_params=pltpu.CompilerParams(vmem_limit_bytes=40 * 2**20),
    )(values, phases, potential)


def exchange(values):
    return lax.all_to_all(values, "fft", split_axis=0, concat_axis=0, tiled=True)


def per_device(
    orbitals,
    response,
    residual,
    old_direction,
    old_norm,
    band_energy,
    kinetic,
    form_factor,
    sphere_index,
    atom_positions,
    proj_atom,
    coupling,
    potential,
):
    groups = lax.axis_size("fft")
    pools = lax.axis_size("kpool")
    bands = orbitals.shape[1]
    points = sphere_index.shape[1]
    columns = points // STICK_LEN
    slab = NG // groups
    atoms = atom_positions.shape[1]
    channels = form_factor.shape[2]
    share = atoms // groups
    cells = NG * NG
    scale = 2.0 / (pools * points * groups)
    lines = jnp.asarray(line_matrix(columns))

    own = sphere_index[0].reshape(columns, STICK_LEN)[:, 0] // NG
    res_now = residual[0]
    first = jnp.concatenate(
        [
            jnp.sum(res_now * res_now, axis=(1, 2)),
            (own // NG).astype(jnp.float32),
            (own % NG).astype(jnp.float32),
        ]
    )
    first = exchange(jnp.broadcast_to(first[None], (groups, first.shape[0])))
    norm_now = jnp.sum(first[:, :bands], axis=0)
    col_x = first[:, bands : bands + columns].reshape(-1).astype(jnp.int32)
    col_y = first[:, bands + columns :].reshape(-1).astype(jnp.int32)
    phases = column_phases(col_x, col_y)
    direction = res_now + (norm_now / old_norm[0])[:, None, None] * old_direction[0]

    index = sphere_index[0]
    theta = TWO_PI * (
        atom_positions[0][:, None] * signed(index // cells)[None, :]
        + atom_positions[1][:, None] * signed(index // NG % NG)[None, :]
        + atom_positions[2][:, None] * signed(index % NG)[None, :]
    )
    cosine, sine = jnp.cos(theta)[:, None, :], jnp.sin(theta)[:, None, :]
    real_part, imag_part = form_factor[0, 0][None], form_factor[0, 1][None]
    tabs = jnp.stack(
        [real_part * cosine + imag_part * sine, imag_part * cosine - real_part * sine]
    ).reshape(2 * atoms * channels, points)
    slots = proj_atom.reshape(channels, -1)
    number = jnp.sum(
        (slots[None] == jnp.arange(atoms, dtype=jnp.int32)[:, None, None]).astype(jnp.float32), axis=2
    )

    fields = jnp.concatenate([orbitals, response, direction[None]], 0)
    sent = lax.dot_general(
        lines, fields.reshape(6 * bands, 2 * points), (((1,), (1,)), ((), ())), precision=HIGH
    )
    amps = lax.dot_general(
        tabs, direction.reshape(4 * bands, points), (((1,), (1,)), ((), ())), precision=HIGH
    ).reshape(2, atoms, channels, 2 * bands, 2)
    amps = jnp.stack(
        [amps[0, ..., 0] + amps[1, ..., 1], amps[0, ..., 1] - amps[1, ..., 0]], 1
    )
    chunk = slab * 2 * columns * 6 * bands
    got = exchange(
        jnp.concatenate([sent.reshape(groups, chunk), amps.reshape(groups, -1)], axis=1)
    )
    values = got[:, :chunk].reshape(groups, slab, 2, columns, 3, bands, 2)
    values = jnp.transpose(values, (1, 4, 6, 5, 2, 0, 3)).reshape(slab * 6 * bands, -1)
    sticks, curve, base, slope = planes(values, phases, potential, bands)
    curve = jnp.sum(curve, axis=1) / (NG * cells)

    me = lax.axis_index("fft")
    mine = lax.dynamic_slice_in_dim(number, me * share, share, 0)
    summed = jnp.sum(got[:, chunk:], axis=0).reshape(share, 2, channels, bands, 2)
    summed = summed * mine[:, None, :, None, None]
    herm_real = (0.5 * (coupling[0] + coupling[0].T)).reshape(2, channels, 2, channels)
    herm_imag = (0.5 * (coupling[1] - coupling[1].T)).reshape(2, channels, 2, channels)
    mixing = jnp.stack(
        [jnp.stack([herm_real, -herm_imag], 0), jnp.stack([herm_imag, herm_real], 0)], 0
    )
    mixed = contract("pqscte,aqent->apcns", mixing, summed)
    curve = curve + jnp.sum(mixed * summed, axis=(0, 1, 2, 4))
    local = kinetic[0][None, :] - band_energy[0][:, None]
    curve = curve + jnp.sum(local[:, None, :] * direction * direction, axis=(1, 2))
    mixed = (mixed * mine[:, None, :, None, None]).reshape(1, -1)

    sticks = sticks.reshape(slab, 2, bands, 2, groups, columns)
    sticks = jnp.transpose(sticks, (4, 2, 1, 0, 3, 5)).reshape(groups, -1)
    width = sticks.shape[1]
    shared = jnp.concatenate([mixed, curve[None]], axis=1)
    back = exchange(
        jnp.concatenate([sticks, jnp.broadcast_to(shared, (groups, shared.shape[1]))], axis=1)
    )
    curvature = jnp.sum(back[:, -bands:], axis=0)
    sticks = back[:, :width].reshape(groups, 2 * bands, -1)
    sticks = jnp.transpose(sticks, (1, 0, 2)).reshape(2 * bands, -1)
    potential_term = jnp.dot(sticks, lines, precision=HIGH).reshape(bands, 4, points) / (NG * cells)
    coupled = back[:, width:-bands].reshape(atoms, 2, channels, 2 * bands)
    coupled = jnp.transpose(coupled, (1, 3, 0, 2)).reshape(2, 2 * bands, atoms * channels)
    weights = jnp.stack(
        [
            jnp.stack([coupled[0], -coupled[1]], 1),
            jnp.stack([coupled[1], coupled[0]], 1),
        ],
        1,
    ).reshape(4 * bands, 2 * atoms * channels)
    nonlocal_term = jnp.dot(weights, tabs, precision=HIGH).reshape(bands, 4, points)
    image = local[:, None, :] * direction + potential_term + nonlocal_term
    step = norm_now / (curvature + SMALL_TERM)
    next_response = response[0] + step[:, None, None] * direction
    next_residual = res_now - step[:, None, None] * image
    density = (base + jnp.sum(slope * step[None, None, :, None], axis=2)) * scale
    if pools == 2:
        density = density + lax.ppermute(density, "kpool", [(0, 1), (1, 0)])
    else:
        density = lax.psum(density, "kpool")
    return (next_response[None], next_residual[None], direction[None], density)


def solution(mesh):
    in_specs = (
        P("kpool", None, None, "fft"),
        P("kpool", None, None, "fft"),
        P("kpool", None, None, "fft"),
        P("kpool", None, None, "fft"),
        P("kpool", None),
        P("kpool", None),
        P("kpool", "fft"),
        P("kpool", None, None, "fft"),
        P("kpool", "fft"),
        P(),
        P(),
        P(),
        P(None, "fft", None),
    )
    out_specs = (
        P("kpool", None, None, "fft"),
        P("kpool", None, None, "fft"),
        P("kpool", None, None, "fft"),
        P(None, "fft", None),
    )
    return jax.shard_map(
        per_device, mesh=mesh, in_specs=in_specs, out_specs=out_specs, check_vma=False
    )
```

```python
import functools
import math

import jax
import jax.numpy as jnp
import numpy as np
from jax import lax
from jax.experimental import pallas as pl
from jax.experimental.pallas import tpu as pltpu
from jax.sharding import PartitionSpec as P

NG = 64
STICK_LEN = 32

TWO_PI = 2.0 * math.pi
SMALL_TERM = 1e-06
LANES = 128
FIRST, ENDS, LINES, AMPS, BACK, SHARE = range(6)


def line_matrix(columns, groups):
    slab = NG // groups
    depth = (np.arange(STICK_LEN) - STICK_LEN // 2) % NG
    angle = 2.0 * np.pi / NG * (np.outer(np.arange(NG), depth) % NG)
    cosine, sine = np.cos(angle), np.sin(angle)
    parts = np.stack([np.stack([cosine, -sine], 1), np.stack([sine, cosine], 1)], 1)
    parts = parts.reshape(groups, slab, 2, 2, STICK_LEN)
    full = np.einsum("gzdct,SR->dzgScRt", parts, np.eye(columns))
    full = full.reshape(NG * 2 * columns, 2 * columns * STICK_LEN).astype(np.float32)
    high = full.astype(jnp.bfloat16)
    low = (full - high.astype(np.float32)).astype(jnp.bfloat16)
    return high, low


def signed(values):
    return jnp.where(values < NG // 2, values, values - NG).astype(jnp.float32)


def split(values):
    high = values.astype(jnp.bfloat16)
    return high, (values - high.astype(jnp.float32)).astype(jnp.bfloat16)


def product(left, right, dims):
    def one(a, b):
        return lax.dot_general(a, b, (dims, ((), ())), preferred_element_type=jnp.float32)

    return one(left[0], right[0]) + (one(left[0], right[1]) + one(left[1], right[0]))


def widen(blocks):
    total = sum(block.shape[1] for block in blocks)
    if total < LANES:
        blocks = blocks + [jnp.zeros((blocks[0].shape[0], LANES - total), jnp.float32)]
    return jnp.concatenate(blocks, axis=1)


def step_kernel(
    groups, pools, scale,
    orbitals_ref, response_ref, residual_ref, previous_ref, bands_ref, kinetic_ref, form_ref,
    wound_ref, cosine_ref, sine_ref, number_ref, mixing_ref, potential_ref, line_high, line_low,
    next_response_ref, next_residual_ref, direction_ref, density_ref,
    first_out, first_in, ends_out, ends_in, lines_out, lines_in, amps_out, amps_in,
    back_out, back_in, share_out, share_in, send_sems, recv_sems,
    tab_high, tab_low, carry, turn, high, low, values_high, values_low,
    sticks, curve, slope, pair_out, pair_in, pair_send, pair_recv,
):
    me = lax.axis_index("fft")
    bands = orbitals_ref.shape[0]
    points = orbitals_ref.shape[2]
    columns = points // STICK_LEN
    slab = NG // groups
    cells = NG * NG
    channels = form_ref.shape[1]
    atoms = cosine_ref.shape[0]
    share = atoms // groups
    count = groups * columns
    block = 2 * bands
    tile = high.shape[1] // 2
    steps = cells // tile

    def peer(k):
        return lax.rem(me + k, groups)

    def copy(stage, source, target, other):
        return pltpu.make_async_remote_copy(
            src_ref=source,
            dst_ref=target.at[me],
            send_sem=send_sems.at[stage, other],
            recv_sem=recv_sems.at[stage, me],
            device_id={"fft": other},
            device_id_type=pl.DeviceIdType.MESH,
        )

    def each_peer(action):
        def run(k, _):
            action(peer(k))
            return 0

        lax.fori_loop(1, groups, run, 0)

    def send(stage, out, target, own=False):
        each_peer(lambda other: copy(stage, out if own else out.at[other], target, other).start())
        target[me] = out[...] if own else out[me]

    def arrive(stage, target):
        def action(other):
            pltpu.make_async_remote_copy(
                src_ref=target.at[other],
                dst_ref=target.at[other],
                send_sem=send_sems.at[stage, other],
                recv_sem=recv_sems.at[stage, other],
                device_id={"fft": other},
                device_id_type=pl.DeviceIdType.MESH,
            ).wait_recv()

        each_peer(action)

    barrier = pltpu.get_barrier_semaphore()
    each_peer(
        lambda other: pl.semaphore_signal(
            barrier, inc=1, device_id={"fft": other}, device_id_type=pl.DeviceIdType.MESH
        )
    )
    if pools == 2:
        partner = {"kpool": 1 - lax.axis_index("kpool")}
        pl.semaphore_signal(
            barrier, inc=1, device_id=partner, device_id_type=pl.DeviceIdType.MESH
        )

    norm = jnp.zeros((bands, points), jnp.float32)
    for part in range(4):
        norm = norm + residual_ref[:, part, :] * residual_ref[:, part, :]
    norm = jnp.sum(norm, axis=1, keepdims=True)
    first_out[0] = jnp.broadcast_to(norm, (bands, LANES))
    first_out[1] = wound_ref[...]
    pl.semaphore_wait(barrier, groups - 1 + (1 if pools == 2 else 0))
    send(FIRST, first_out, first_in, own=True)

    lines = (line_high[...], line_low[...])

    def to_lines(rows):
        made = product(lines, split(jnp.concatenate(rows, axis=0)), ((1,), (1,)))
        out = []
        for field in range(len(rows) // 2):
            cuts = [
                made[k * count : (k + 1) * count, field * block : (field + 1) * block]
                for k in range(2 * slab)
            ]
            out.append(widen(cuts).reshape(groups, columns, LANES))
        return out

    def spin_rows(parts):
        return [jnp.concatenate(parts[0:2], axis=1), jnp.concatenate(parts[2:4], axis=1)]

    made = to_lines(
        spin_rows([orbitals_ref[:, part, :] for part in range(4)])
        + spin_rows([response_ref[:, part, :] for part in range(4)])
    )
    ends_out[:, 0] = made[0]
    ends_out[:, 1] = made[1]
    send(ENDS, ends_out, ends_in)

    def fill(group, _):
        for inner in range(share):
            atom = group * share + inner
            c = cosine_ref[pl.ds(atom, 1), :]
            s = sine_ref[pl.ds(atom, 1), :]
            real = split(form_ref[0] * c + form_ref[1] * s)
            imag = split(form_ref[1] * c - form_ref[0] * s)
            row = pl.ds(pl.multiple_of((inner * groups + group) * channels, channels), channels)
            for out, re, im in zip((tab_high, tab_low), real, imag):
                out[row, 0:points] = re
                out[row, points:] = im
        return 0

    lax.fori_loop(0, groups, fill, 0)

    arrive(FIRST, first_in)
    norm = jnp.sum(first_in[:, 0], axis=0)[:, 0:1]
    ratio = norm / bands_ref[0, :, 0:1]
    direction = []
    for part in range(4):
        value = residual_ref[:, part, :] + ratio * previous_ref[:, part, :]
        direction_ref[:, part, :] = value
        direction.append(value)
    lines_out[...] = to_lines(spin_rows(direction))[0]
    send(LINES, lines_out, lines_in)

    plain = jnp.concatenate([direction[0], direction[2], direction[1], direction[3]], axis=0)
    crossed = jnp.concatenate([direction[1], direction[3], -direction[0], -direction[2]], axis=0)
    amps = product(
        (tab_high[...], tab_low[...]),
        split(jnp.concatenate([plain, crossed], axis=1)),
        ((1,), (1,)),
    )
    rows = groups * channels
    amps = widen([amps[k * rows : (k + 1) * rows] for k in range(share)])
    amps_out[...] = amps.reshape(groups, channels, LANES)
    send(AMPS, amps_out, amps_in)

    wound = first_in[:, 1].reshape(count, LANES)
    ahead = jnp.broadcast_to(2.0 * (wound[:, NG : NG + 1] - wound[:, 0:1]), wound.shape)
    carry[0] = jnp.cos(TWO_PI / NG * wound)
    carry[1] = jnp.sin(TWO_PI / NG * wound)
    turn[0] = jnp.cos(TWO_PI / NG * ahead)
    turn[1] = jnp.sin(TWO_PI / NG * ahead)
    local = kinetic_ref[...] - bands_ref[1, :, 0:1]
    own_curve = jnp.zeros((bands, points), jnp.float32)
    for value in direction:
        own_curve = own_curve + local * value * value
    own_curve = jnp.sum(own_curve, axis=1, keepdims=True)
    sticks[...] = jnp.zeros_like(sticks)
    curve[...] = jnp.zeros_like(curve)

    arrive(ENDS, ends_in)
    arrive(LINES, lines_in)
    height = slab * block
    for field in range(3):
        got = lines_in[...] if field == 2 else ends_in[:, field]
        got = got.reshape(count, LANES).T
        got = jnp.concatenate([got[0:height], got[height : 2 * height]], axis=1)
        parts = split(got)
        values_high[field * height : (field + 1) * height] = parts[0]
        values_low[field * height : (field + 1) * height] = parts[1]

    def plane_step(index, _):
        place = pl.ds(pl.multiple_of(index * tile, tile), tile)
        for pair in range(tile // LANES):
            cosine, sine = carry[0], carry[1]
            left, right = pair * LANES, tile + pair * LANES
            for out, c, s in zip((high, low), split(cosine), split(sine)):
                out[0:count, left : left + LANES] = c
                out[0:count, right : right + LANES] = s
                out[count:, left : left + LANES] = -s
                out[count:, right : right + LANES] = c
            carry[0] = cosine * turn[0] - sine * turn[1]
            carry[1] = sine * turn[0] + cosine * turn[1]

        table = (high[...], low[...])
        grid = product((values_high[...], values_low[...]), table, ((1,), (0,)))
        total = curve[...]
        fields = []
        for z in range(slab):

            def part(field, spin):
                row = ((field * slab + z) * 2 + spin) * bands
                cut = grid[row : row + bands]
                return cut[:, :tile], cut[:, tile:]

            (ur, ui), (dr, di) = part(0, 0), part(0, 1)

            def terms(up, down):
                (pr, pi), (qr, qi) = up, down
                same_up = ur * pr + ui * pi
                same_down = dr * qr + di * qi
                return (
                    same_up + same_down,
                    ur * qr + ui * qi + dr * pr + di * pi,
                    ur * qi - ui * qr - (dr * pi - di * pr),
                    same_up - same_down,
                )

            (pr, pi), (qr, qi) = part(2, 0), part(2, 1)
            for mu, value in enumerate(terms(part(1, 0), part(1, 1))):
                row = mu * slab + z
                pair_out[row : row + 1, place] = jnp.sum(value, axis=0, keepdims=True)
            for mu, value in enumerate(terms((pr, pi), (qr, qi))):
                slope[mu * slab + z, :, place] = value
            scalar, bx, by, bz = (potential_ref[k, z : z + 1, place] for k in range(4))
            upper, lower = scalar + bz, scalar - bz
            new_pr = upper * pr + bx * qr + by * qi
            new_pi = upper * pi + bx * qi - by * qr
            new_qr = bx * pr - by * pi + lower * qr
            new_qi = bx * pi + by * pr + lower * qi
            total = total + (pr * new_pr + pi * new_pi + qr * new_qr + qi * new_qi)
            fields.append(jnp.concatenate([new_pr, new_pi], axis=1))
            fields.append(jnp.concatenate([new_qr, new_qi], axis=1))
        curve[...] = total
        sticks[...] += product(table, split(jnp.concatenate(fields, axis=0)), ((1,), (1,)))
        return 0

    lax.fori_loop(0, steps // 2, plane_step, 0)

    arrive(AMPS, amps_in)
    summed = jnp.sum(amps_in[...], axis=0) * number_ref[...]
    mixed_all = product(split(mixing_ref[...]), split(summed), ((1,), (0,)))
    spot = lax.broadcasted_iota(jnp.int32, (channels, LANES), 1) // bands % 4
    mixed = jnp.zeros((channels, LANES), jnp.float32)
    for v in range(4):
        for u in range(4):
            row = (v * 4 + u) * channels
            moved = mixed_all[row : row + channels]
            if u != v:
                moved = pltpu.roll(moved, bands * (u - v) % LANES, 1)
            mixed = mixed + jnp.where(spot == u, moved, 0.0)
    share_out[0:channels] = mixed * number_ref[...]
    pairing = jnp.broadcast_to(jnp.sum(mixed * summed, axis=0, keepdims=True), (bands, LANES))
    lane = lax.broadcasted_iota(jnp.int32, (bands, LANES), 1) % bands
    row = lax.broadcasted_iota(jnp.int32, (bands, LANES), 0)
    own_curve = own_curve + jnp.sum(jnp.where(lane == row, pairing, 0.0), axis=1, keepdims=True)
    send(SHARE, share_out, share_in, own=True)

    lax.fori_loop(steps // 2, steps, plane_step, 0)

    own_curve = own_curve + jnp.sum(curve[...], axis=1, keepdims=True) / (NG * cells)
    made = widen([sticks[0:count], sticks[count:]])
    back_out[:, 0] = made.reshape(groups, columns, LANES)
    back_out[:, 1] = jnp.broadcast_to(
        jnp.broadcast_to(own_curve, (bands, LANES))[None], (groups, bands, LANES)
    )
    send(BACK, back_out, back_in)

    arrive(SHARE, share_in)
    coupled = share_in[...].reshape(groups * channels, LANES).T
    coupled = jnp.concatenate(
        [coupled[k * 2 * block : (k + 1) * 2 * block] for k in range(share)], axis=1
    )
    with_tabs = product(split(coupled), (tab_high[...], tab_low[...]), ((1,), (0,)))
    added_real = with_tabs[0:block, 0:points] - with_tabs[block:, points:]
    added_imag = with_tabs[block:, 0:points] + with_tabs[0:block, points:]
    arrive(BACK, back_in)
    curvature = jnp.sum(back_in[:, 1], axis=0)[:, 0:1]
    step = norm / (curvature + SMALL_TERM)

    for half in range(2):
        for row in range(half * 2 * slab, (half + 1) * 2 * slab):
            moved = jnp.sum(slope[row] * step, axis=0, keepdims=True)
            pair_out[row : row + 1, :] = (pair_out[row : row + 1, :] + moved) * scale
        if pools == 2:
            part = pl.ds(half * 2 * slab, 2 * slab)
            pltpu.make_async_remote_copy(
                src_ref=pair_out.at[part],
                dst_ref=pair_in.at[part],
                send_sem=pair_send.at[half],
                recv_sem=pair_recv.at[half],
                device_id=partner,
                device_id_type=pl.DeviceIdType.MESH,
            ).start()

    got = back_in[:, 0].reshape(count, LANES).T
    got = jnp.concatenate([got[k * block : (k + 1) * block] for k in range(2 * slab)], axis=1)
    term = product(split(got), lines, ((1,), (0,))) / (NG * cells)
    for part in range(4):
        spin = part // 2
        added = (added_real, added_imag)[part % 2][spin * bands : (spin + 1) * bands]
        placed = term[spin * bands : (spin + 1) * bands, part % 2 * points : (part % 2 + 1) * points]
        value = direction_ref[:, part, :]
        image = local * value + placed + added
        next_response_ref[:, part, :] = response_ref[:, part, :] + step * value
        next_residual_ref[:, part, :] = residual_ref[:, part, :] - step * image

    for half in range(2):
        if pools == 2:
            part = pl.ds(half * 2 * slab, 2 * slab)
            pltpu.make_async_remote_copy(
                src_ref=pair_out.at[part],
                dst_ref=pair_in.at[part],
                send_sem=pair_send.at[half],
                recv_sem=pair_recv.at[half],
                device_id=partner,
                device_id_type=pl.DeviceIdType.MESH,
            ).wait()
        for mu in range(2 * half, 2 * half + 2):
            value = pair_out[mu * slab : (mu + 1) * slab]
            if pools == 2:
                value = value + pair_in[mu * slab : (mu + 1) * slab]
            density_ref[mu] = value

    def sent(other):
        copy(FIRST, first_out, first_in, other).wait_send()
        copy(ENDS, ends_out.at[other], ends_in, other).wait_send()
        copy(LINES, lines_out.at[other], lines_in, other).wait_send()
        copy(AMPS, amps_out.at[other], amps_in, other).wait_send()
        copy(BACK, back_out.at[other], back_in, other).wait_send()
        copy(SHARE, share_out, share_in, other).wait_send()

    each_peer(sent)


def per_device(
    orbitals,
    response,
    residual,
    old_direction,
    old_norm,
    band_energy,
    kinetic,
    form_factor,
    sphere_index,
    atom_positions,
    proj_atom,
    coupling,
    potential,
):
    groups = lax.axis_size("fft")
    pools = lax.axis_size("kpool")
    bands = orbitals.shape[1]
    points = sphere_index.shape[1]
    columns = points // STICK_LEN
    slab = NG // groups
    atoms = atom_positions.shape[1]
    channels = form_factor.shape[2]
    share = atoms // groups
    cells = NG * NG
    count = groups * columns
    tile = 8 * NG
    scale = 2.0 / (pools * points * groups)
    line_high, line_low = line_matrix(columns, groups)

    index = sphere_index[0]
    own = index.reshape(columns, STICK_LEN)[:, 0:1] // NG
    lanes = jnp.arange(LANES, dtype=jnp.int32)[None, :]
    wound = ((own // NG * (lanes // NG) + own % NG * (lanes % NG)) % NG).astype(jnp.float32)
    theta = TWO_PI * (
        atom_positions[0][:, None] * signed(index // cells)[None, :]
        + atom_positions[1][:, None] * signed(index // NG % NG)[None, :]
        + atom_positions[2][:, None] * signed(index % NG)[None, :]
    )
    slots = proj_atom.reshape(channels, -1)
    held = lax.axis_index("fft") * share + lanes // (4 * bands)
    number = jnp.sum((slots[:, :, None] == held[None]).astype(jnp.float32), axis=1)
    herm_real = (0.5 * (coupling[0] + coupling[0].T)).reshape(2, channels, 2, channels)
    herm_imag = (0.5 * (coupling[1] - coupling[1].T)).reshape(2, channels, 2, channels)
    mixing = jnp.stack(
        [jnp.stack([herm_real, -herm_imag], 0), jnp.stack([herm_imag, herm_real], 0)], 0
    )
    mixing = jnp.transpose(mixing, (1, 4, 0, 2, 3, 5)).reshape(16 * channels, channels)
    per_band = jnp.broadcast_to(jnp.stack([old_norm[0], band_energy[0]])[:, :, None], (2, bands, LANES))

    def vmem(*shape):
        return pltpu.VMEM(shape, jnp.float32)

    def half(*shape):
        return pltpu.VMEM(shape, jnp.bfloat16)

    field = jax.ShapeDtypeStruct(orbitals.shape[1:], jnp.float32)
    out = pl.pallas_call(
        functools.partial(step_kernel, groups, pools, scale),
        out_shape=[field, field, field, jax.ShapeDtypeStruct(potential.shape, jnp.float32)],
        in_specs=[pl.BlockSpec(memory_space=pltpu.VMEM)] * 15,
        out_specs=[pl.BlockSpec(memory_space=pltpu.VMEM)] * 4,
        scratch_shapes=[
            vmem(2, 8, LANES),
            vmem(groups, 2, 8, LANES),
            vmem(groups, 2, columns, LANES),
            vmem(groups, 2, columns, LANES),
            vmem(groups, columns, LANES),
            vmem(groups, columns, LANES),
            vmem(groups, channels, LANES),
            vmem(groups, channels, LANES),
            vmem(groups, 2, columns, LANES),
            vmem(groups, 2, columns, LANES),
            vmem(channels, LANES),
            vmem(groups, channels, LANES),
            pltpu.SemaphoreType.DMA((6, groups)),
            pltpu.SemaphoreType.DMA((6, groups)),
            half(atoms * channels, 2 * points),
            half(atoms * channels, 2 * points),
            vmem(2, count, LANES),
            vmem(2, count, LANES),
            half(2 * count, 2 * tile),
            half(2 * count, 2 * tile),
            half(6 * bands * slab, 2 * count),
            half(6 * bands * slab, 2 * count),
            vmem(2 * count, 2 * bands * slab),
            vmem(bands, tile),
            vmem(4 * slab, bands, cells),
            vmem(4 * slab, cells),
            vmem(4 * slab, cells),
            pltpu.SemaphoreType.DMA((2,)),
            pltpu.SemaphoreType.DMA((2,)),
        ],
        compiler_params=pltpu.CompilerParams(
            collective_id=0, has_side_effects=True, vmem_limit_bytes=48 * 2**20
        ),
    )(
        orbitals[0], response[0], residual[0], old_direction[0], per_band, kinetic, form_factor[0],
        wound, jnp.cos(theta), jnp.sin(theta), number, mixing, potential,
        jnp.asarray(line_high), jnp.asarray(line_low),
    )
    density = out[3]
    if pools != 2:
        density = lax.psum(density, "kpool")
    return (out[0][None], out[1][None], out[2][None], density)


def solution(mesh):
    in_specs = (
        P("kpool", None, None, "fft"),
        P("kpool", None, None, "fft"),
        P("kpool", None, None, "fft"),
        P("kpool", None, None, "fft"),
        P("kpool", None),
        P("kpool", None),
        P("kpool", "fft"),
        P("kpool", None, None, "fft"),
        P("kpool", "fft"),
        P(),
        P(),
        P(),
        P(None, "fft", None),
    )
    out_specs = (
        P("kpool", None, None, "fft"),
        P("kpool", None, None, "fft"),
        P("kpool", None, None, "fft"),
        P(None, "fft", None),
    )
    return jax.shard_map(
        per_device, mesh=mesh, in_specs=in_specs, out_specs=out_specs, check_vma=False
    )
```

```python
import functools
import math

import jax
import jax.numpy as jnp
import numpy as np
from jax import lax
from jax.experimental import pallas as pl
from jax.experimental.pallas import tpu as pltpu
from jax.sharding import PartitionSpec as P

NG = 64
STICK_LEN = 32

TWO_PI = 2.0 * math.pi
SMALL_TERM = 1e-06
LANES = 128
FIRST, ENDS, LINES, AMPS, BACK, SHARE = range(6)


def line_matrix(columns, groups):
    slab = NG // groups
    depth = (np.arange(STICK_LEN) - STICK_LEN // 2) % NG
    angle = 2.0 * np.pi / NG * (np.outer(np.arange(NG), depth) % NG)
    cosine, sine = np.cos(angle), np.sin(angle)
    parts = np.stack([np.stack([cosine, -sine], 1), np.stack([sine, cosine], 1)], 1)
    parts = parts.reshape(groups, slab, 2, 2, STICK_LEN)
    full = np.einsum("gzdct,SR->dzgScRt", parts, np.eye(columns))
    full = full.reshape(NG * 2 * columns, 2 * columns * STICK_LEN).astype(np.float32)
    high = full.astype(jnp.bfloat16)
    low = (full - high.astype(np.float32)).astype(jnp.bfloat16)
    return high, low


def signed(values):
    return jnp.where(values < NG // 2, values, values - NG).astype(jnp.float32)


def split(values):
    high = values.astype(jnp.bfloat16)
    return high, (values - high.astype(jnp.float32)).astype(jnp.bfloat16)


def product(left, right, dims):
    def one(a, b):
        return lax.dot_general(a, b, (dims, ((), ())), preferred_element_type=jnp.float32)

    return one(left[0], right[0]) + (one(left[0], right[1]) + one(left[1], right[0]))


def widen(blocks):
    total = sum(block.shape[1] for block in blocks)
    if total < LANES:
        blocks = blocks + [jnp.zeros((blocks[0].shape[0], LANES - total), jnp.float32)]
    return jnp.concatenate(blocks, axis=1)


def step_kernel(
    groups, pools, scale,
    orbitals_ref, response_ref, residual_ref, previous_ref, old_ref, energy_ref, kinetic_ref,
    form_ref, index_ref, atoms_ref, slots_ref, coupling_ref, potential_far, line_far,
    next_response_ref, next_residual_ref, direction_ref, density_ref,
    first_out, first_in, ends_out, ends_in, lines_out, lines_in, amps_out, amps_in,
    back_out, back_in, share_out, share_in, send_sems, recv_sems,
    tab_high, tab_low, carry, turn, table, values,
    cosine_ref, sine_ref, potential_ref, line_ref, near,
    sticks, curve, slope, pair_out, pair_in, pair_send, pair_recv,
):
    me = lax.axis_index("fft")
    bands = orbitals_ref.shape[0]
    points = orbitals_ref.shape[2]
    columns = points // STICK_LEN
    slab = NG // groups
    cells = NG * NG
    channels = form_ref.shape[1]
    atoms = atoms_ref.shape[1]
    share = atoms // groups
    count = groups * columns
    block = 2 * bands
    tile = table.shape[1] // 2
    steps = cells // tile

    def peer(k):
        return lax.rem(me + k, groups)

    def copy(stage, source, target, other):
        return pltpu.make_async_remote_copy(
            src_ref=source,
            dst_ref=target.at[me],
            send_sem=send_sems.at[stage, other],
            recv_sem=recv_sems.at[stage, me],
            device_id={"fft": other},
            device_id_type=pl.DeviceIdType.MESH,
        )

    def each_peer(action):
        def run(k, _):
            action(peer(k))
            return 0

        lax.fori_loop(1, groups, run, 0)

    def send(stage, out, target, own=False):
        each_peer(lambda other: copy(stage, out if own else out.at[other], target, other).start())
        target[me] = out[...] if own else out[me]

    def arrive(stage, target):
        def action(other):
            pltpu.make_async_remote_copy(
                src_ref=target.at[other],
                dst_ref=target.at[other],
                send_sem=send_sems.at[stage, other],
                recv_sem=recv_sems.at[stage, other],
                device_id={"fft": other},
                device_id_type=pl.DeviceIdType.MESH,
            ).wait_recv()

        each_peer(action)

    line_copy = pltpu.make_async_copy(line_far, line_ref, near.at[0])
    potential_copy = pltpu.make_async_copy(potential_far, potential_ref, near.at[1])
    line_copy.start()
    potential_copy.start()
    barrier = pltpu.get_barrier_semaphore()
    each_peer(
        lambda other: pl.semaphore_signal(
            barrier, inc=1, device_id={"fft": other}, device_id_type=pl.DeviceIdType.MESH
        )
    )
    if pools == 2:
        partner = {"kpool": 1 - lax.axis_index("kpool")}
        pl.semaphore_signal(
            barrier, inc=1, device_id=partner, device_id_type=pl.DeviceIdType.MESH
        )

    norm = jnp.zeros((bands, points), jnp.float32)
    for part in range(4):
        norm = norm + residual_ref[:, part, :] * residual_ref[:, part, :]
    norm = jnp.sum(norm, axis=1, keepdims=True)
    first_out[0] = jnp.broadcast_to(norm, (bands, LANES))
    digits = NG.bit_length() - 1
    index = index_ref[...]
    spot = lax.broadcasted_iota(jnp.int32, (columns, points), 1)
    row = lax.broadcasted_iota(jnp.int32, (columns, points), 0) * STICK_LEN
    heads = jnp.where(spot == row, jnp.broadcast_to(index, (columns, points)), 0)

    def head(values):
        return jnp.sum(values.astype(jnp.float32), axis=1, keepdims=True).astype(jnp.int32)

    lane = lax.broadcasted_iota(jnp.int32, (columns, LANES), 1)
    over, down = lane >> digits, lane & (NG - 1)
    wound = head(heads >> (2 * digits)) * over + head((heads >> digits) & (NG - 1)) * down
    first_out[1] = (wound & (NG - 1)).astype(jnp.float32)

    def upright(values):
        size = values.shape[1]
        across = lax.broadcasted_iota(jnp.int32, (size, size), 1)
        along = lax.broadcasted_iota(jnp.int32, (size, size), 0)
        spread = jnp.where(across == along, jnp.broadcast_to(values, (size, size)), 0.0)
        return jnp.sum(spread, axis=1, keepdims=True)

    theta = jnp.zeros((atoms, points), jnp.float32)
    for axis in range(3):
        freq = signed((index >> ((2 - axis) * digits)) & (NG - 1))
        theta = theta + upright(atoms_ref[axis : axis + 1, :]) * freq
    theta = TWO_PI * theta
    cosine_ref[...] = jnp.cos(theta)
    sine_ref[...] = jnp.sin(theta)
    old_norm = upright(old_ref[...])
    energy = upright(energy_ref[...])
    pl.semaphore_wait(barrier, groups - 1 + (1 if pools == 2 else 0))
    send(FIRST, first_out, first_in, own=True)

    line_copy.wait()
    lines = (line_ref[0], line_ref[1])

    def to_lines(rows):
        made = product(lines, split(jnp.concatenate(rows, axis=0)), ((1,), (1,)))
        out = []
        for field in range(len(rows) // 2):
            cuts = [
                made[k * count : (k + 1) * count, field * block : (field + 1) * block]
                for k in range(2 * slab)
            ]
            out.append(widen(cuts).reshape(groups, columns, LANES))
        return out

    def spin_rows(parts):
        return [jnp.concatenate(parts[0:2], axis=1), jnp.concatenate(parts[2:4], axis=1)]

    made = to_lines(
        spin_rows([orbitals_ref[:, part, :] for part in range(4)])
        + spin_rows([response_ref[:, part, :] for part in range(4)])
    )
    ends_out[:, 0] = made[0]
    ends_out[:, 1] = made[1]
    send(ENDS, ends_out, ends_in)

    def fill(group, _):
        for inner in range(share):
            atom = group * share + inner
            c = cosine_ref[pl.ds(atom, 1), :]
            s = sine_ref[pl.ds(atom, 1), :]
            real = split(form_ref[0] * c + form_ref[1] * s)
            imag = split(form_ref[1] * c - form_ref[0] * s)
            row = pl.ds(pl.multiple_of((inner * groups + group) * channels, channels), channels)
            for out, re, im in zip((tab_high, tab_low), real, imag):
                out[row, 0:points] = re
                out[row, points:] = im
        return 0

    lax.fori_loop(0, groups, fill, 0)

    arrive(FIRST, first_in)
    norm = jnp.sum(first_in[:, 0], axis=0)[:, 0:1]
    ratio = norm / old_norm
    direction = []
    for part in range(4):
        value = residual_ref[:, part, :] + ratio * previous_ref[:, part, :]
        direction_ref[:, part, :] = value
        direction.append(value)
    lines_out[...] = to_lines(spin_rows(direction))[0]
    send(LINES, lines_out, lines_in)

    plain = jnp.concatenate([direction[0], direction[2], direction[1], direction[3]], axis=0)
    crossed = jnp.concatenate([direction[1], direction[3], -direction[0], -direction[2]], axis=0)
    amps = product(
        (tab_high[...], tab_low[...]),
        split(jnp.concatenate([plain, crossed], axis=1)),
        ((1,), (1,)),
    )
    rows = groups * channels
    amps = widen([amps[k * rows : (k + 1) * rows] for k in range(share)])
    amps_out[...] = amps.reshape(groups, channels, LANES)
    send(AMPS, amps_out, amps_in)

    wound = first_in[:, 1].reshape(count, LANES)
    ahead = jnp.broadcast_to(2.0 * (wound[:, NG : NG + 1] - wound[:, 0:1]), wound.shape)
    carry[0] = jnp.cos(TWO_PI / NG * wound)
    carry[1] = jnp.sin(TWO_PI / NG * wound)
    turn[0] = jnp.cos(TWO_PI / NG * ahead)
    turn[1] = jnp.sin(TWO_PI / NG * ahead)
    local = kinetic_ref[...] - energy
    own_curve = jnp.zeros((bands, points), jnp.float32)
    for value in direction:
        own_curve = own_curve + local * value * value
    own_curve = jnp.sum(own_curve, axis=1, keepdims=True)
    sticks[...] = jnp.zeros_like(sticks)
    curve[...] = jnp.zeros_like(curve)

    arrive(ENDS, ends_in)
    arrive(LINES, lines_in)
    height = slab * block
    for field in range(3):
        got = lines_in[...] if field == 2 else ends_in[:, field]
        got = got.reshape(count, LANES).T
        got = jnp.concatenate([got[0:height], got[height : 2 * height]], axis=1)
        parts = split(got)
        values[field * height : (field + 1) * height] = jnp.concatenate(
            [parts[0], parts[0], parts[1]], axis=1
        )

    def plane_step(index, _):
        place = pl.ds(pl.multiple_of(index * tile, tile), tile)
        for pair in range(tile // LANES):
            cosine, sine = carry[0], carry[1]
            left, right = pair * LANES, tile + pair * LANES
            for k, c, s in zip((0, 1), split(cosine), split(sine)):
                for base in (0, 4 * count) if k == 0 else (2 * count,):
                    table[base : base + count, left : left + LANES] = c
                    table[base : base + count, right : right + LANES] = s
                    table[base + count : base + 2 * count, left : left + LANES] = -s
                    table[base + count : base + 2 * count, right : right + LANES] = c
            carry[0] = cosine * turn[0] - sine * turn[1]
            carry[1] = sine * turn[0] + cosine * turn[1]

        grid = jnp.dot(values[...], table[...], preferred_element_type=jnp.float32)
        total = curve[...]
        fields = []
        for z in range(slab):

            def part(field, spin):
                row = ((field * slab + z) * 2 + spin) * bands
                cut = grid[row : row + bands]
                return cut[:, :tile], cut[:, tile:]

            (ur, ui), (dr, di) = part(0, 0), part(0, 1)

            def terms(up, down):
                (pr, pi), (qr, qi) = up, down
                same_up = ur * pr + ui * pi
                same_down = dr * qr + di * qi
                return (
                    same_up + same_down,
                    ur * qr + ui * qi + dr * pr + di * pi,
                    ur * qi - ui * qr - (dr * pi - di * pr),
                    same_up - same_down,
                )

            (pr, pi), (qr, qi) = part(2, 0), part(2, 1)
            for mu, value in enumerate(terms(part(1, 0), part(1, 1))):
                row = mu * slab + z
                pair_out[row : row + 1, place] = jnp.sum(value, axis=0, keepdims=True)
            for mu, value in enumerate(terms((pr, pi), (qr, qi))):
                slope[mu * slab + z, :, place] = value
            scalar, bx, by, bz = (potential_ref[k, z : z + 1, place] for k in range(4))
            upper, lower = scalar + bz, scalar - bz
            new_pr = upper * pr + bx * qr + by * qi
            new_pi = upper * pi + bx * qi - by * qr
            new_qr = bx * pr - by * pi + lower * qr
            new_qi = bx * pi + by * pr + lower * qi
            total = total + (pr * new_pr + pi * new_pi + qr * new_qr + qi * new_qi)
            fields.append(jnp.concatenate([new_pr, new_pi], axis=1))
            fields.append(jnp.concatenate([new_qr, new_qi], axis=1))
        curve[...] = total
        pieces = (table[0 : 2 * count], table[2 * count : 4 * count])
        sticks[...] += product(pieces, split(jnp.concatenate(fields, axis=0)), ((1,), (1,)))
        return 0

    potential_copy.wait()
    lax.fori_loop(0, steps // 2, plane_step, 0)

    arrive(AMPS, amps_in)
    holder = lax.broadcasted_iota(jnp.int32, (channels, LANES), 1) // (4 * bands)
    number = jnp.zeros((channels, LANES), jnp.float32)
    for inner in range(share):
        found = (slots_ref[...] == me * share + inner).astype(jnp.float32)
        found = jnp.sum(found, axis=1, keepdims=True)
        number = number + jnp.where(holder == inner, found, 0.0)
    summed = jnp.sum(amps_in[...], axis=0) * number
    herm_real = 0.5 * (coupling_ref[0] + coupling_ref[0].T)
    herm_imag = 0.5 * (coupling_ref[1] - coupling_ref[1].T)
    whole = ((herm_real, -herm_imag), (herm_imag, herm_real))
    mixing = jnp.concatenate(
        [
            whole[u // 2][v // 2][
                u % 2 * channels : (u % 2 + 1) * channels, v % 2 * channels : (v % 2 + 1) * channels
            ]
            for v in range(4)
            for u in range(4)
        ],
        axis=0,
    )
    mixed_all = product(split(mixing), split(summed), ((1,), (0,)))
    spot = lax.broadcasted_iota(jnp.int32, (channels, LANES), 1) // bands % 4
    mixed = jnp.zeros((channels, LANES), jnp.float32)
    for v in range(4):
        for u in range(4):
            row = (v * 4 + u) * channels
            moved = mixed_all[row : row + channels]
            if u != v:
                moved = pltpu.roll(moved, bands * (u - v) % LANES, 1)
            mixed = mixed + jnp.where(spot == u, moved, 0.0)
    share_out[0:channels] = mixed * number
    pairing = jnp.broadcast_to(jnp.sum(mixed * summed, axis=0, keepdims=True), (bands, LANES))
    lane = lax.broadcasted_iota(jnp.int32, (bands, LANES), 1) % bands
    row = lax.broadcasted_iota(jnp.int32, (bands, LANES), 0)
    own_curve = own_curve + jnp.sum(jnp.where(lane == row, pairing, 0.0), axis=1, keepdims=True)
    send(SHARE, share_out, share_in, own=True)

    lax.fori_loop(steps // 2, steps, plane_step, 0)

    own_curve = own_curve + jnp.sum(curve[...], axis=1, keepdims=True) / (NG * cells)
    made = widen([sticks[0:count], sticks[count:]])
    back_out[:, 0] = made.reshape(groups, columns, LANES)
    back_out[:, 1] = jnp.broadcast_to(
        jnp.broadcast_to(own_curve, (bands, LANES))[None], (groups, bands, LANES)
    )
    send(BACK, back_out, back_in)

    arrive(SHARE, share_in)
    coupled = share_in[...].reshape(groups * channels, LANES).T
    coupled = jnp.concatenate(
        [coupled[k * 2 * block : (k + 1) * 2 * block] for k in range(share)], axis=1
    )
    with_tabs = product(split(coupled), (tab_high[...], tab_low[...]), ((1,), (0,)))
    added_real = with_tabs[0:block, 0:points] - with_tabs[block:, points:]
    added_imag = with_tabs[block:, 0:points] + with_tabs[0:block, points:]
    arrive(BACK, back_in)
    curvature = jnp.sum(back_in[:, 1], axis=0)[:, 0:1]
    step = norm / (curvature + SMALL_TERM)

    for half in range(2):
        for row in range(half * 2 * slab, (half + 1) * 2 * slab):
            moved = jnp.sum(slope[row] * step, axis=0, keepdims=True)
            pair_out[row : row + 1, :] = (pair_out[row : row + 1, :] + moved) * scale
        if pools == 2:
            part = pl.ds(half * 2 * slab, 2 * slab)
            pltpu.make_async_remote_copy(
                src_ref=pair_out.at[part],
                dst_ref=pair_in.at[part],
                send_sem=pair_send.at[half],
                recv_sem=pair_recv.at[half],
                device_id=partner,
                device_id_type=pl.DeviceIdType.MESH,
            ).start()

    got = back_in[:, 0].reshape(count, LANES).T
    got = jnp.concatenate([got[k * block : (k + 1) * block] for k in range(2 * slab)], axis=1)
    term = product(split(got), lines, ((1,), (0,))) / (NG * cells)
    for part in range(4):
        spin = part // 2
        added = (added_real, added_imag)[part % 2][spin * bands : (spin + 1) * bands]
        placed = term[spin * bands : (spin + 1) * bands, part % 2 * points : (part % 2 + 1) * points]
        value = direction_ref[:, part, :]
        image = local * value + placed + added
        next_response_ref[:, part, :] = response_ref[:, part, :] + step * value
        next_residual_ref[:, part, :] = residual_ref[:, part, :] - step * image

    for half in range(2):
        if pools == 2:
            part = pl.ds(half * 2 * slab, 2 * slab)
            pltpu.make_async_remote_copy(
                src_ref=pair_out.at[part],
                dst_ref=pair_in.at[part],
                send_sem=pair_send.at[half],
                recv_sem=pair_recv.at[half],
                device_id=partner,
                device_id_type=pl.DeviceIdType.MESH,
            ).wait()
        for mu in range(2 * half, 2 * half + 2):
            value = pair_out[mu * slab : (mu + 1) * slab]
            if pools == 2:
                value = value + pair_in[mu * slab : (mu + 1) * slab]
            density_ref[mu] = value

    def sent(other):
        copy(FIRST, first_out, first_in, other).wait_send()
        copy(ENDS, ends_out.at[other], ends_in, other).wait_send()
        copy(LINES, lines_out.at[other], lines_in, other).wait_send()
        copy(AMPS, amps_out.at[other], amps_in, other).wait_send()
        copy(BACK, back_out.at[other], back_in, other).wait_send()
        copy(SHARE, share_out, share_in, other).wait_send()

    each_peer(sent)


def per_device(
    orbitals,
    response,
    residual,
    old_direction,
    old_norm,
    band_energy,
    kinetic,
    form_factor,
    sphere_index,
    atom_positions,
    proj_atom,
    coupling,
    potential,
):
    groups = lax.axis_size("fft")
    pools = lax.axis_size("kpool")
    bands = orbitals.shape[1]
    points = sphere_index.shape[1]
    columns = points // STICK_LEN
    slab = NG // groups
    atoms = atom_positions.shape[1]
    channels = form_factor.shape[2]
    cells = NG * NG
    count = groups * columns
    tile = 8 * NG
    scale = 2.0 / (pools * points * groups)
    lines = jnp.asarray(np.stack(line_matrix(columns, groups)))

    def vmem(*shape):
        return pltpu.VMEM(shape, jnp.float32)

    def half(*shape):
        return pltpu.VMEM(shape, jnp.bfloat16)

    field = jax.ShapeDtypeStruct(orbitals.shape[1:], jnp.float32)
    out = pl.pallas_call(
        functools.partial(step_kernel, groups, pools, scale),
        out_shape=[field, field, field, jax.ShapeDtypeStruct(potential.shape, jnp.float32)],
        in_specs=[pl.BlockSpec(memory_space=pltpu.VMEM)] * 12 + [pl.BlockSpec(memory_space=pltpu.HBM)] * 2,
        out_specs=[pl.BlockSpec(memory_space=pltpu.VMEM)] * 4,
        scratch_shapes=[
            vmem(2, 8, LANES),
            vmem(groups, 2, 8, LANES),
            vmem(groups, 2, columns, LANES),
            vmem(groups, 2, columns, LANES),
            vmem(groups, columns, LANES),
            vmem(groups, columns, LANES),
            vmem(groups, channels, LANES),
            vmem(groups, channels, LANES),
            vmem(groups, 2, columns, LANES),
            vmem(groups, 2, columns, LANES),
            vmem(channels, LANES),
            vmem(groups, channels, LANES),
            pltpu.SemaphoreType.DMA((6, groups)),
            pltpu.SemaphoreType.DMA((6, groups)),
            half(atoms * channels, 2 * points),
            half(atoms * channels, 2 * points),
            vmem(2, count, LANES),
            vmem(2, count, LANES),
            half(6 * count, 2 * tile),
            half(6 * bands * slab, 6 * count),
            vmem(atoms, points),
            vmem(atoms, points),
            vmem(*potential.shape),
            half(*lines.shape),
            pltpu.SemaphoreType.DMA((2,)),
            vmem(2 * count, 2 * bands * slab),
            vmem(bands, tile),
            vmem(4 * slab, bands, cells),
            vmem(4 * slab, cells),
            vmem(4 * slab, cells),
            pltpu.SemaphoreType.DMA((2,)),
            pltpu.SemaphoreType.DMA((2,)),
        ],
        compiler_params=pltpu.CompilerParams(
            collective_id=0, has_side_effects=True, vmem_limit_bytes=48 * 2**20
        ),
    )(
        orbitals[0], response[0], residual[0], old_direction[0], old_norm, band_energy, kinetic,
        form_factor[0], sphere_index, atom_positions, proj_atom.reshape(channels, -1), coupling,
        potential, lines,
    )
    density = out[3]
    if pools != 2:
        density = lax.psum(density, "kpool")
    return (out[0][None], out[1][None], out[2][None], density)


def solution(mesh):
    in_specs = (
        P("kpool", None, None, "fft"),
        P("kpool", None, None, "fft"),
        P("kpool", None, None, "fft"),
        P("kpool", None, None, "fft"),
        P("kpool", None),
        P("kpool", None),
        P("kpool", "fft"),
        P("kpool", None, None, "fft"),
        P("kpool", "fft"),
        P(),
        P(),
        P(),
        P(None, "fft", None),
    )
    out_specs = (
        P("kpool", None, None, "fft"),
        P("kpool", None, None, "fft"),
        P("kpool", None, None, "fft"),
        P(None, "fft", None),
    )
    return jax.shard_map(
        per_device, mesh=mesh, in_specs=in_specs, out_specs=out_specs, check_vma=False
    )
```

```python
import functools
import math

import jax
import jax.numpy as jnp
import numpy as np
from jax import lax
from jax.experimental import pallas as pl
from jax.experimental.pallas import tpu as pltpu
from jax.sharding import PartitionSpec as P

NG = 64
STICK_LEN = 32

TWO_PI = 2.0 * math.pi
SMALL_TERM = 1e-06
LANES = 128
FIRST, ENDS, LINES, AMPS, BACK, SHARE = range(6)


def line_matrix(columns, groups):
    slab = NG // groups
    depth = (np.arange(STICK_LEN) - STICK_LEN // 2) % NG
    angle = 2.0 * np.pi / NG * (np.outer(np.arange(NG), depth) % NG)
    cosine, sine = np.cos(angle), np.sin(angle)
    parts = np.stack([np.stack([cosine, -sine], 1), np.stack([sine, cosine], 1)], 1)
    parts = parts.reshape(groups, slab, 2, 2, STICK_LEN)
    full = np.einsum("gzdct,SR->dzgScRt", parts, np.eye(columns))
    full = full.reshape(NG * 2 * columns, 2 * columns * STICK_LEN).astype(np.float32)
    high = full.astype(jnp.bfloat16)
    low = (full - high.astype(np.float32)).astype(jnp.bfloat16)
    return high, low


def signed(values):
    return jnp.where(values < NG // 2, values, values - NG).astype(jnp.float32)


def split(values):
    high = values.astype(jnp.bfloat16)
    return high, (values - high.astype(jnp.float32)).astype(jnp.bfloat16)


def product(left, right, dims):
    def one(a, b):
        return lax.dot_general(a, b, (dims, ((), ())), preferred_element_type=jnp.float32)

    return one(left[0], right[0]) + (one(left[0], right[1]) + one(left[1], right[0]))


def widen(blocks):
    total = sum(block.shape[1] for block in blocks)
    if total < LANES:
        blocks = blocks + [jnp.zeros((blocks[0].shape[0], LANES - total), jnp.float32)]
    return jnp.concatenate(blocks, axis=1)


def step_kernel(
    groups, pools, scale,
    orbitals_ref, response_ref, residual_ref, previous_ref, old_ref, energy_ref, kinetic_ref,
    form_ref, index_ref, atoms_ref, slots_ref, coupling_ref, potential_far, line_far,
    next_response_ref, next_residual_ref, direction_ref, density_ref,
    first_out, first_in, ends_out, ends_in, lines_out, lines_in, amps_out, amps_in,
    back_out, back_in, share_out, share_in, send_sems, recv_sems,
    tab_high, tab_low, carry, turn, table, values,
    cosine_ref, sine_ref, potential_ref, line_ref, near,
    sticks, curve, slope, pair_out, pair_in, pair_send, pair_recv,
):
    me = lax.axis_index("fft")
    bands = orbitals_ref.shape[0]
    points = orbitals_ref.shape[2]
    columns = points // STICK_LEN
    slab = NG // groups
    cells = NG * NG
    channels = form_ref.shape[1]
    atoms = atoms_ref.shape[1]
    share = atoms // groups
    count = groups * columns
    block = 2 * bands
    tile = table.shape[1] // 2
    steps = cells // tile

    def peer(k):
        return lax.rem(me + k, groups)

    def copy(stage, source, target, other):
        return pltpu.make_async_remote_copy(
            src_ref=source,
            dst_ref=target.at[me],
            send_sem=send_sems.at[stage, other],
            recv_sem=recv_sems.at[stage, me],
            device_id={"fft": other},
            device_id_type=pl.DeviceIdType.MESH,
        )

    def each_peer(action):
        def run(k, _):
            action(peer(k))
            return 0

        lax.fori_loop(1, groups, run, 0)

    def send(stage, out, target, own=False):
        each_peer(lambda other: copy(stage, out if own else out.at[other], target, other).start())
        target[me] = out[...] if own else out[me]

    def arrive(stage, target):
        def action(other):
            pltpu.make_async_remote_copy(
                src_ref=target.at[other],
                dst_ref=target.at[other],
                send_sem=send_sems.at[stage, other],
                recv_sem=recv_sems.at[stage, other],
                device_id={"fft": other},
                device_id_type=pl.DeviceIdType.MESH,
            ).wait_recv()

        each_peer(action)

    line_copy = pltpu.make_async_copy(line_far, line_ref, near.at[0])
    potential_copy = pltpu.make_async_copy(potential_far, potential_ref, near.at[1])
    line_copy.start()
    potential_copy.start()
    barrier = pltpu.get_barrier_semaphore()
    each_peer(
        lambda other: pl.semaphore_signal(
            barrier, inc=1, device_id={"fft": other}, device_id_type=pl.DeviceIdType.MESH
        )
    )
    if pools == 2:
        partner = {"kpool": 1 - lax.axis_index("kpool")}
        pl.semaphore_signal(
            barrier, inc=1, device_id=partner, device_id_type=pl.DeviceIdType.MESH
        )

    norm = jnp.zeros((bands, points), jnp.float32)
    for part in range(4):
        norm = norm + residual_ref[:, part, :] * residual_ref[:, part, :]
    norm = jnp.sum(norm, axis=1, keepdims=True)
    first_out[0] = jnp.broadcast_to(norm, (bands, LANES))
    digits = NG.bit_length() - 1
    index = index_ref[...]
    spot = lax.broadcasted_iota(jnp.int32, (columns, points), 1)
    row = lax.broadcasted_iota(jnp.int32, (columns, points), 0) * STICK_LEN
    heads = jnp.where(spot == row, jnp.broadcast_to(index, (columns, points)), 0)

    def head(values):
        return jnp.sum(values.astype(jnp.float32), axis=1, keepdims=True).astype(jnp.int32)

    lane = lax.broadcasted_iota(jnp.int32, (columns, LANES), 1)
    over, down = lane >> digits, lane & (NG - 1)
    wound = head(heads >> (2 * digits)) * over + head((heads >> digits) & (NG - 1)) * down
    first_out[1] = (wound & (NG - 1)).astype(jnp.float32)

    def upright(values):
        size = values.shape[1]
        across = lax.broadcasted_iota(jnp.int32, (size, size), 1)
        along = lax.broadcasted_iota(jnp.int32, (size, size), 0)
        spread = jnp.where(across == along, jnp.broadcast_to(values, (size, size)), 0.0)
        return jnp.sum(spread, axis=1, keepdims=True)

    theta = jnp.zeros((atoms, points), jnp.float32)
    for axis in range(3):
        freq = signed((index >> ((2 - axis) * digits)) & (NG - 1))
        theta = theta + upright(atoms_ref[axis : axis + 1, :]) * freq
    theta = TWO_PI * theta
    cosine_ref[...] = jnp.cos(theta)
    sine_ref[...] = jnp.sin(theta)
    old_norm = upright(old_ref[...])
    energy = upright(energy_ref[...])
    pl.semaphore_wait(barrier, groups - 1 + (1 if pools == 2 else 0))
    send(FIRST, first_out, first_in, own=True)

    line_copy.wait()
    lines = (line_ref[0], line_ref[1])

    def to_lines(rows):
        made = product(lines, split(jnp.concatenate(rows, axis=0)), ((1,), (1,)))
        out = []
        for field in range(len(rows) // 2):
            cuts = [
                made[k * count : (k + 1) * count, field * block : (field + 1) * block]
                for k in range(2 * slab)
            ]
            out.append(widen(cuts).reshape(groups, columns, LANES))
        return out

    def spin_rows(parts):
        return [jnp.concatenate(parts[0:2], axis=1), jnp.concatenate(parts[2:4], axis=1)]

    made = to_lines(
        spin_rows([orbitals_ref[:, part, :] for part in range(4)])
        + spin_rows([response_ref[:, part, :] for part in range(4)])
    )
    ends_out[:, 0] = made[0]
    ends_out[:, 1] = made[1]
    send(ENDS, ends_out, ends_in)

    def fill(group, _):
        for inner in range(share):
            atom = group * share + inner
            c = cosine_ref[pl.ds(atom, 1), :]
            s = sine_ref[pl.ds(atom, 1), :]
            real = split(form_ref[0] * c + form_ref[1] * s)
            imag = split(form_ref[1] * c - form_ref[0] * s)
            row = pl.ds(pl.multiple_of((inner * groups + group) * channels, channels), channels)
            for out, re, im in zip((tab_high, tab_low), real, imag):
                out[row, 0:points] = re
                out[row, points:] = im
        return 0

    lax.fori_loop(0, groups, fill, 0)

    arrive(FIRST, first_in)
    norm = jnp.sum(first_in[:, 0], axis=0)[:, 0:1]
    ratio = norm / old_norm
    direction = []
    for part in range(4):
        value = residual_ref[:, part, :] + ratio * previous_ref[:, part, :]
        direction_ref[:, part, :] = value
        direction.append(value)
    lines_out[...] = to_lines(spin_rows(direction))[0]
    send(LINES, lines_out, lines_in)

    plain = jnp.concatenate([direction[0], direction[2], direction[1], direction[3]], axis=0)
    crossed = jnp.concatenate([direction[1], direction[3], -direction[0], -direction[2]], axis=0)
    amps = product(
        (tab_high[...], tab_low[...]),
        split(jnp.concatenate([plain, crossed], axis=1)),
        ((1,), (1,)),
    )
    rows = groups * channels
    amps = widen([amps[k * rows : (k + 1) * rows] for k in range(share)])
    amps_out[...] = amps.reshape(groups, channels, LANES)
    send(AMPS, amps_out, amps_in)

    wound = first_in[:, 1].reshape(count, LANES)
    ahead = jnp.broadcast_to(2.0 * (wound[:, NG : NG + 1] - wound[:, 0:1]), wound.shape)
    carry[0] = jnp.cos(TWO_PI / NG * wound)
    carry[1] = jnp.sin(TWO_PI / NG * wound)
    turn[0] = jnp.cos(TWO_PI / NG * ahead)
    turn[1] = jnp.sin(TWO_PI / NG * ahead)
    local = kinetic_ref[...] - energy
    own_curve = jnp.zeros((bands, points), jnp.float32)
    for value in direction:
        own_curve = own_curve + local * value * value
    own_curve = jnp.sum(own_curve, axis=1, keepdims=True)
    sticks[...] = jnp.zeros_like(sticks)
    curve[...] = jnp.zeros_like(curve)

    arrive(ENDS, ends_in)
    arrive(LINES, lines_in)
    height = slab * block
    for field in range(3):
        got = lines_in[...] if field == 2 else ends_in[:, field]
        got = got.reshape(count, LANES).T
        got = jnp.concatenate([got[0:height], got[height : 2 * height]], axis=1)
        parts = split(got)
        values[field * height : (field + 1) * height] = jnp.concatenate(
            [parts[0], parts[0], parts[1]], axis=1
        )

    def plane_step(index, _):
        place = pl.ds(pl.multiple_of(index * tile, tile), tile)
        for pair in range(tile // LANES):
            cosine, sine = carry[0], carry[1]
            left, right = pair * LANES, tile + pair * LANES
            for k, c, s in zip((0, 1), split(cosine), split(sine)):
                for base in (0, 4 * count) if k == 0 else (2 * count,):
                    table[base : base + count, left : left + LANES] = c
                    table[base : base + count, right : right + LANES] = s
                    table[base + count : base + 2 * count, left : left + LANES] = -s
                    table[base + count : base + 2 * count, right : right + LANES] = c
            carry[0] = cosine * turn[0] - sine * turn[1]
            carry[1] = sine * turn[0] + cosine * turn[1]

        grid = jnp.dot(values[...], table[...], preferred_element_type=jnp.float32)
        total = curve[...]
        fields = []
        for z in range(slab):

            def part(field, spin):
                row = ((field * slab + z) * 2 + spin) * bands
                cut = grid[row : row + bands]
                return cut[:, :tile], cut[:, tile:]

            (ur, ui), (dr, di) = part(0, 0), part(0, 1)

            def terms(up, down):
                (pr, pi), (qr, qi) = up, down
                same_up = ur * pr + ui * pi
                same_down = dr * qr + di * qi
                return (
                    same_up + same_down,
                    ur * qr + ui * qi + dr * pr + di * pi,
                    ur * qi - ui * qr - (dr * pi - di * pr),
                    same_up - same_down,
                )

            (pr, pi), (qr, qi) = part(2, 0), part(2, 1)
            for mu, value in enumerate(terms(part(1, 0), part(1, 1))):
                row = mu * slab + z
                pair_out[row : row + 1, place] = jnp.sum(value, axis=0, keepdims=True)
            for mu, value in enumerate(terms((pr, pi), (qr, qi))):
                slope[mu * slab + z, :, place] = value
            scalar, bx, by, bz = (potential_ref[k, z : z + 1, place] for k in range(4))
            upper, lower = scalar + bz, scalar - bz
            new_pr = upper * pr + bx * qr + by * qi
            new_pi = upper * pi + bx * qi - by * qr
            new_qr = bx * pr - by * pi + lower * qr
            new_qi = bx * pi + by * pr + lower * qi
            total = total + (pr * new_pr + pi * new_pi + qr * new_qr + qi * new_qi)
            fields.append(jnp.concatenate([new_pr, new_pi], axis=1))
            fields.append(jnp.concatenate([new_qr, new_qi], axis=1))
        curve[...] = total
        pieces = (table[0 : 2 * count], table[2 * count : 4 * count])
        sticks[...] += product(pieces, split(jnp.concatenate(fields, axis=0)), ((1,), (1,)))
        return 0

    potential_copy.wait()
    lax.fori_loop(0, steps // 2, plane_step, 0)

    arrive(AMPS, amps_in)
    holder = lax.broadcasted_iota(jnp.int32, (channels, LANES), 1) // (4 * bands)
    number = jnp.zeros((channels, LANES), jnp.float32)
    for inner in range(share):
        found = (slots_ref[...] == me * share + inner).astype(jnp.float32)
        found = jnp.sum(found, axis=1, keepdims=True)
        number = number + jnp.where(holder == inner, found, 0.0)
    summed = jnp.sum(amps_in[...], axis=0) * number
    herm_real = 0.5 * (coupling_ref[0] + coupling_ref[0].T)
    herm_imag = 0.5 * (coupling_ref[1] - coupling_ref[1].T)
    whole = ((herm_real, -herm_imag), (herm_imag, herm_real))
    mixing = jnp.concatenate(
        [
            whole[u // 2][v // 2][
                u % 2 * channels : (u % 2 + 1) * channels, v % 2 * channels : (v % 2 + 1) * channels
            ]
            for v in range(4)
            for u in range(4)
        ],
        axis=0,
    )
    mixed_all = product(split(mixing), split(summed), ((1,), (0,)))
    spot = lax.broadcasted_iota(jnp.int32, (channels, LANES), 1) // bands % 4
    mixed = jnp.zeros((channels, LANES), jnp.float32)
    for v in range(4):
        for u in range(4):
            row = (v * 4 + u) * channels
            moved = mixed_all[row : row + channels]
            if u != v:
                moved = pltpu.roll(moved, bands * (u - v) % LANES, 1)
            mixed = mixed + jnp.where(spot == u, moved, 0.0)
    share_out[0:channels] = mixed * number
    pairing = jnp.broadcast_to(jnp.sum(mixed * summed, axis=0, keepdims=True), (bands, LANES))
    lane = lax.broadcasted_iota(jnp.int32, (bands, LANES), 1) % bands
    row = lax.broadcasted_iota(jnp.int32, (bands, LANES), 0)
    own_curve = own_curve + jnp.sum(jnp.where(lane == row, pairing, 0.0), axis=1, keepdims=True)
    send(SHARE, share_out, share_in, own=True)

    lax.fori_loop(steps // 2, steps, plane_step, 0)

    own_curve = own_curve + jnp.sum(curve[...], axis=1, keepdims=True) / (NG * cells)
    made = widen([sticks[0:count], sticks[count:]])
    back_out[:, 0] = made.reshape(groups, columns, LANES)
    back_out[:, 1] = jnp.broadcast_to(
        jnp.broadcast_to(own_curve, (bands, LANES))[None], (groups, bands, LANES)
    )
    send(BACK, back_out, back_in)

    arrive(SHARE, share_in)
    coupled = share_in[...].reshape(groups * channels, LANES).T
    coupled = jnp.concatenate(
        [coupled[k * 2 * block : (k + 1) * 2 * block] for k in range(share)], axis=1
    )
    with_tabs = product(split(coupled), (tab_high[...], tab_low[...]), ((1,), (0,)))
    added_real = with_tabs[0:block, 0:points] - with_tabs[block:, points:]
    added_imag = with_tabs[block:, 0:points] + with_tabs[0:block, points:]
    arrive(BACK, back_in)
    curvature = jnp.sum(back_in[:, 1], axis=0)[:, 0:1]
    step = norm / (curvature + SMALL_TERM)

    for half in range(2):
        for row in range(half * 2 * slab, (half + 1) * 2 * slab):
            moved = jnp.sum(slope[row] * step, axis=0, keepdims=True)
            pair_out[row : row + 1, :] = (pair_out[row : row + 1, :] + moved) * scale
        if pools == 2:
            part = pl.ds(half * 2 * slab, 2 * slab)
            pltpu.make_async_remote_copy(
                src_ref=pair_out.at[part],
                dst_ref=pair_in.at[part],
                send_sem=pair_send.at[half],
                recv_sem=pair_recv.at[half],
                device_id=partner,
                device_id_type=pl.DeviceIdType.MESH,
            ).start()

    got = back_in[:, 0].reshape(count, LANES).T
    got = jnp.concatenate([got[k * block : (k + 1) * block] for k in range(2 * slab)], axis=1)
    term = product(split(got), lines, ((1,), (0,))) / (NG * cells)
    for part in range(4):
        spin = part // 2
        added = (added_real, added_imag)[part % 2][spin * bands : (spin + 1) * bands]
        placed = term[spin * bands : (spin + 1) * bands, part % 2 * points : (part % 2 + 1) * points]
        value = direction_ref[:, part, :]
        image = local * value + placed + added
        next_response_ref[:, part, :] = response_ref[:, part, :] + step * value
        next_residual_ref[:, part, :] = residual_ref[:, part, :] - step * image

    for half in range(2):
        if pools == 2:
            part = pl.ds(half * 2 * slab, 2 * slab)
            pltpu.make_async_remote_copy(
                src_ref=pair_out.at[part],
                dst_ref=pair_in.at[part],
                send_sem=pair_send.at[half],
                recv_sem=pair_recv.at[half],
                device_id=partner,
                device_id_type=pl.DeviceIdType.MESH,
            ).wait()
        for mu in range(2 * half, 2 * half + 2):
            value = pair_out[mu * slab : (mu + 1) * slab]
            if pools == 2:
                value = value + pair_in[mu * slab : (mu + 1) * slab]
            density_ref[mu] = value

    def sent(other):
        copy(FIRST, first_out, first_in, other).wait_send()
        copy(ENDS, ends_out.at[other], ends_in, other).wait_send()
        copy(LINES, lines_out.at[other], lines_in, other).wait_send()
        copy(AMPS, amps_out.at[other], amps_in, other).wait_send()
        copy(BACK, back_out.at[other], back_in, other).wait_send()
        copy(SHARE, share_out, share_in, other).wait_send()

    each_peer(sent)


def staged_kernel(groups, pools, scale, *refs):
    far, rest, near, sems = refs[:12], refs[12:-13], refs[-13:-1], refs[-1]
    copies = [pltpu.make_async_copy(a, b, sems.at[k]) for k, (a, b) in enumerate(zip(far, near))]
    for one in copies:
        one.start()
    for one in copies:
        one.wait()
    step_kernel(groups, pools, scale, *near, *rest)


def per_device(
    orbitals,
    response,
    residual,
    old_direction,
    old_norm,
    band_energy,
    kinetic,
    form_factor,
    sphere_index,
    atom_positions,
    proj_atom,
    coupling,
    potential,
):
    groups = lax.axis_size("fft")
    pools = lax.axis_size("kpool")
    bands = orbitals.shape[1]
    points = sphere_index.shape[1]
    columns = points // STICK_LEN
    slab = NG // groups
    atoms = atom_positions.shape[1]
    channels = form_factor.shape[2]
    cells = NG * NG
    count = groups * columns
    tile = 8 * NG
    scale = 2.0 / (pools * points * groups)
    lines = jnp.asarray(np.stack(line_matrix(columns, groups)))

    def vmem(*shape):
        return pltpu.VMEM(shape, jnp.float32)

    def half(*shape):
        return pltpu.VMEM(shape, jnp.bfloat16)

    inputs = (
        orbitals[0], response[0], residual[0], old_direction[0], old_norm, band_energy, kinetic,
        form_factor[0], sphere_index, atom_positions, proj_atom.reshape(channels, -1), coupling,
    )
    field = jax.ShapeDtypeStruct(orbitals.shape[1:], jnp.float32)
    out = pl.pallas_call(
        functools.partial(staged_kernel, groups, pools, scale),
        out_shape=[field, field, field, jax.ShapeDtypeStruct(potential.shape, jnp.float32)],
        in_specs=[pl.BlockSpec(memory_space=pltpu.HBM)] * 14,
        out_specs=[pl.BlockSpec(memory_space=pltpu.VMEM)] * 4,
        scratch_shapes=[
            vmem(2, 8, LANES),
            vmem(groups, 2, 8, LANES),
            vmem(groups, 2, columns, LANES),
            vmem(groups, 2, columns, LANES),
            vmem(groups, columns, LANES),
            vmem(groups, columns, LANES),
            vmem(groups, channels, LANES),
            vmem(groups, channels, LANES),
            vmem(groups, 2, columns, LANES),
            vmem(groups, 2, columns, LANES),
            vmem(channels, LANES),
            vmem(groups, channels, LANES),
            pltpu.SemaphoreType.DMA((6, groups)),
            pltpu.SemaphoreType.DMA((6, groups)),
            half(atoms * channels, 2 * points),
            half(atoms * channels, 2 * points),
            vmem(2, count, LANES),
            vmem(2, count, LANES),
            half(6 * count, 2 * tile),
            half(6 * bands * slab, 6 * count),
            vmem(atoms, points),
            vmem(atoms, points),
            vmem(*potential.shape),
            half(*lines.shape),
            pltpu.SemaphoreType.DMA((2,)),
            vmem(2 * count, 2 * bands * slab),
            vmem(bands, tile),
            vmem(4 * slab, bands, cells),
            vmem(4 * slab, cells),
            vmem(4 * slab, cells),
            pltpu.SemaphoreType.DMA((2,)),
            pltpu.SemaphoreType.DMA((2,)),
        ]
        + [pltpu.VMEM(one.shape, one.dtype) for one in inputs]
        + [pltpu.SemaphoreType.DMA((len(inputs),))],
        compiler_params=pltpu.CompilerParams(
            collective_id=0, has_side_effects=True, vmem_limit_bytes=48 * 2**20
        ),
    )(*inputs, potential, lines)
    density = out[3]
    if pools != 2:
        density = lax.psum(density, "kpool")
    return (out[0][None], out[1][None], out[2][None], density)


def solution(mesh):
    in_specs = (
        P("kpool", None, None, "fft"),
        P("kpool", None, None, "fft"),
        P("kpool", None, None, "fft"),
        P("kpool", None, None, "fft"),
        P("kpool", None),
        P("kpool", None),
        P("kpool", "fft"),
        P("kpool", None, None, "fft"),
        P("kpool", "fft"),
        P(),
        P(),
        P(),
        P(None, "fft", None),
    )
    out_specs = (
        P("kpool", None, None, "fft"),
        P("kpool", None, None, "fft"),
        P("kpool", None, None, "fft"),
        P(None, "fft", None),
    )
    return jax.shard_map(
        per_device, mesh=mesh, in_specs=in_specs, out_specs=out_specs, check_vma=False
    )
```
